128 devices in a mesh: ctg: 16 (over y, x), line: 8 (over z, core).
Axes of the slice: x: 4, y: 4, z: 4, core: 2. Of those that a mesh axis runs over, the one named last changes fastest.
Arguments:
- base_flow: float32 [384, 15360], P(None, ('ctg', 'line')), may hold values from -6 to 6
- lodf: bfloat16 [15360, 15360], P('line', 'ctg'), may hold values from -0.3125 to 0.3125
- dual: bfloat16 [15360, 15360], P('line', 'ctg'), may hold values from 0 to 2.5, as said below
- rating: float32 [15360], P('line'), may hold values from 0.3 to 2
- sens: bfloat16 [15360, 2048], P('line', 'ctg'), may hold values from -0.046875 to 0.046875
- fetch_rows: int32 [16, 128, 15], P('ctg'), may hold values from -1 to 119, as said below
- ctg_slot: int32 [15360], P('ctg'), may hold values from 0 to 1919, as said below
Outputs:
- cut: float32 [2048, 384], P(('ctg', 'line'))
The draws below stay inside these ranges and needn't reach their ends.
Inputs may be any that keep to these rules, and one draw needn't show every extreme that they name: `fetch_rows`: -1 marks an empty slot; other entries are distinct columns of flow holder o's block of 120 lines; some pairs (c, o) may have no live slot, and one flow holder has all 15 slots live for every contingency holder. `ctg_slot`: the 960 contingencies of holder c take distinct slots o * 15 + j, exactly the live entries of fetch_rows[c]. `dual`: zero outside the overloaded pairs, positive on them.
All inputs are finite; a program needn't handle non-finite values.
Results may differ from the reference program's by a relative error of at most 0.0059.
Values may be sent and summed in bfloat16 or wider, within the bound.
A program may use at most 64 MiB of HBM per device.

```python
import math
import jax
import jax.numpy as jnp

L = 15360
K_DEV = 960
COLS = 384
K = 15360
J = 2048
L_OWN = 120
CAP = 15
N_CTG = 16
DEVICES = 128


def slot_tables(key):
    seeded = jax.random.fold_in(key, 11)
    key_owner, key_pick, key_order, key_rows = jax.random.split(seeded, 4)
    slot_count = DEVICES * CAP
    full_owner = jax.random.randint(key_owner, (), 0, DEVICES)
    slot_ids = jnp.arange(slot_count, dtype=jnp.int32)
    owner_of = slot_ids // CAP
    forced = owner_of == full_owner
    scores = jax.random.randint(key_pick, (N_CTG, slot_count), 0, 65536) * slot_count + slot_ids[None, :]
    scores = jnp.where(forced[None, :], slot_ids[None, :] - slot_count, scores)
    chosen = jnp.argsort(scores, axis=1, stable=True)[:, :K_DEV].astype(jnp.int32)
    mixing = jax.random.randint(key_order, (N_CTG, K_DEV), 0, 65536) * K_DEV + jnp.arange(K_DEV, dtype=jnp.int32)[None, :]
    shuffle = jnp.argsort(mixing, axis=1, stable=True)
    ctg_table = jnp.take_along_axis(chosen, shuffle, axis=1).reshape(K).astype(jnp.int32)
    taken_mask = jnp.zeros((N_CTG, slot_count), jnp.int32).at[jnp.arange(N_CTG)[:, None], chosen].set(1)
    line_scores = jax.random.randint(key_rows, (N_CTG, DEVICES, L_OWN), 0, 65536) * L_OWN + jnp.arange(L_OWN, dtype=jnp.int32)
    picked = jnp.argsort(line_scores, axis=2, stable=True)[:, :, :CAP].astype(jnp.int32)
    fetch_table = jnp.where(taken_mask.reshape(N_CTG, DEVICES, CAP) == 1, picked, -1).astype(jnp.int32)
    return (fetch_table, ctg_table)


def draw_fetch_rows(key, part):
    return slot_tables(key)[0]


def draw_ctg_slot(key, part):
    return slot_tables(key)[1]


def draw_dual(key, part):
    seeded = jax.random.fold_in(key, 23)
    key_rate, key_mask, key_value = jax.random.split(seeded, 3)
    rate = jnp.exp(jax.random.uniform(key_rate, (1, K), jnp.float32, jnp.log(0.01), jnp.log(0.1)))
    live = jax.random.uniform(key_mask, (L, K), jnp.float32) < rate
    values = jnp.exp(jax.random.uniform(key_value, (L, K), jnp.float32, jnp.log(0.25), jnp.log(2.5)))
    return jnp.where(live, values, 0.0).astype(jnp.bfloat16)


def with_spikes(array, own_key, source, target, shards_of, factor):
    def block_of(axis_at):
        return (jnp.arange(array.shape[axis_at]) // (array.shape[axis_at] // shards_of)).reshape((-1,) + (1,) * (array.ndim - 1 - axis_at))

    near = jax.random.permutation(own_key, shards_of)[block_of(target)]
    second = (block_of(target) + shards_of // 2) % shards_of
    return jnp.where((block_of(source) == near) | (block_of(source) == second), factor * array, array)


def steps_of(rng, extent, pieces, least, top_value):
    factor_of = 1.0
    for dim, parts in pieces:
        steps = jax.random.uniform(jax.random.fold_in(jax.random.fold_in(rng, 6), dim), (parts,), jnp.float32, least / len(pieces), top_value / len(pieces))
        factor_of = factor_of * jnp.repeat(jnp.exp(steps), extent[dim] // parts).reshape((-1,) + (1,) * (len(extent) - 1 - dim))
    return factor_of


def noise(key, shape, deviation, limit, cuts=(), held_as=jnp.bfloat16):
    factor_of = steps_of(key, shape, cuts, -0.22, 0.18) if cuts else 1.0
    values = jax.random.normal(key, shape, jnp.float32) * deviation * factor_of
    return jnp.minimum(jnp.maximum(values, -limit), limit).astype(held_as)


def heavy_noise(stream_key, dims, width, most, cuts, heavy, held_as=jnp.bfloat16):
    drawn = width * jax.random.normal(stream_key, dims, jnp.float32)
    if cuts:
        drawn = drawn * steps_of(stream_key, dims, cuts, -0.22, 0.18)
    return jnp.clip(with_spikes(drawn, jax.random.fold_in(stream_key, 3), *heavy), -most, most).astype(held_as)


def setup_inputs(seed: int = 0) -> dict:
    streams_of = jax.random.split(jax.random.key(seed), 8)
    base_flow = noise(streams_of[0], (COLS, L), 1.0, 6.0, ((1, 128),), jnp.float32)
    lodf = heavy_noise(streams_of[1], (L, K), (K // 20) ** -0.5, 0.3125, ((0, 8), (1, 16)), (1, 0, 16, 2.0))
    dual = draw_dual(jax.random.fold_in(streams_of[7], 71), 0)
    rating = jnp.clip(jnp.exp(math.log(2.0) - 1.89712 * jax.random.uniform(streams_of[3], (L,), jnp.float32) ** steps_of(streams_of[3], (L,), ((0, 8),), -0.2, 0.2)), 0.3, 2.0)
    sens = noise(streams_of[4], (L, J), L ** -0.5, 0.046875, ((0, 8), (1, 16)))
    fetch_rows = draw_fetch_rows(jax.random.fold_in(streams_of[7], 71), 0)
    ctg_slot = draw_ctg_slot(jax.random.fold_in(streams_of[7], 71), 0)
    return {"base_flow": base_flow, "lodf": lodf, "dual": dual, "rating": rating, "sens": sens, "fetch_rows": fetch_rows, "ctg_slot": ctg_slot}


def outage_lines(fetch_rows, ctg_slot):
    owners = jnp.arange(DEVICES, dtype=jnp.int32) * L_OWN
    global_rows = jnp.where(fetch_rows >= 0, fetch_rows + owners[None, :, None], 0)
    global_rows = global_rows.reshape(N_CTG, DEVICES * CAP).astype(jnp.int32)
    wanted = ctg_slot.reshape(N_CTG, K_DEV).astype(jnp.int32)
    return jnp.take_along_axis(global_rows, wanted, axis=1).reshape(K).astype(jnp.int32)


def soft_excess(flow_sum, rating):
    return jnp.sign(flow_sum) * jnp.maximum(jnp.abs(flow_sum) - rating[None, :], 0.0)


def reference(base_flow, lodf, dual, rating, sens, fetch_rows, ctg_slot):
    outage = outage_lines(fetch_rows, ctg_slot)
    outage_flow = jnp.take(base_flow, outage, axis=1).astype(jnp.bfloat16)
    weighted = (dual.astype(jnp.float32) * lodf.astype(jnp.float32)).astype(jnp.bfloat16)
    shift = jnp.dot(outage_flow, weighted.T, preferred_element_type=jnp.float32)
    excess = soft_excess(shift, rating).astype(jnp.bfloat16)
    return jnp.dot(sens.T, excess.T, preferred_element_type=jnp.float32)
```

```python
import jax
import jax.numpy as jnp
from jax import lax
from jax.experimental import pallas as pl
from jax.experimental.pallas import tpu as pltpu
from jax.sharding import PartitionSpec as P

MESH = pl.DeviceIdType.MESH
BF = jnp.bfloat16
F32 = jnp.float32
Q = 384
QH = 192
KD = 960
ML = 1920
MP = 2048
N_SEM = 176


def mod4(v):
    return lax.rem(v + 4, 4)


def kernel(
    fr_h, slot_h, base_h, lodf_h, dual_h, rating_h, sens_h, out_ref,
    fr_v, slot_v, base_v, base_b, lodf_v, dual_v, rating_v, sens_v, w_v,
    ask_s, ask_r, val_s, slots, of_acc, of_b,
    s1, own1, ro1, r1, s2, ro2, r2, ex, cut_acc, cut_v, fin_r,
    load_sem, send_sem, recv_sem,
):
    ctg = lax.axis_index("ctg")
    line = lax.axis_index("line")
    y, x = lax.div(ctg, 4), lax.rem(ctg, 4)
    z, core = lax.div(line, 2), lax.rem(line, 2)
    sent = []

    def device(dy=0, dx=0, dz=0, sibling=False):
        k = 1 - core if sibling else core
        return (mod4(y + dy) * 4 + mod4(x + dx), mod4(z + dz) * 2 + k)

    def send(src, dst, to, now=True):
        i = len(sent)
        copy = pltpu.make_async_remote_copy(
            src_ref=src, dst_ref=dst, send_sem=send_sem.at[i], recv_sem=recv_sem.at[i],
            device_id=to, device_id_type=MESH,
        )
        sent.append(copy)
        copy.start()
        return copy

    loads = {}
    plan = [("fr", fr_h, fr_v.at[0:15]), ("base", base_h, base_v), ("slot", slot_h, slot_v),
            ("lodf", lodf_h, lodf_v), ("dual", dual_h, dual_v), ("sens", sens_h, sens_v.at[0:ML]),
            ("rating", rating_h, rating_v.at[0:15])]
    for i, (name, src, dst) in enumerate(plan):
        loads[name] = pltpu.make_async_copy(src, dst, load_sem.at[i])
        loads[name].start()

    barrier = pltpu.get_barrier_semaphore()
    for s in range(1, 16):
        pl.semaphore_signal(barrier, inc=1, device_id=(lax.rem(ctg + s, 16), line), device_id_type=MESH)
    for s in range(1, 8):
        pl.semaphore_signal(barrier, inc=1, device_id=(ctg, lax.rem(line + s, 8)), device_id_type=MESH)

    loads["fr"].wait()
    row16 = lax.broadcasted_iota(jnp.int32, (16, 128), 0)
    lane16 = lax.broadcasted_iota(jnp.int32, (16, 128), 1)
    table = jnp.where(row16 < 15, fr_v[...], -1).astype(F32)
    ones = jnp.ones((128, 128), BF)
    for c in range(16):
        ask_s[c * 16 : c * 16 + 16, :] = jnp.where(lane16 == c * 8 + line, table, 0.0).astype(BF)
    ask_s[...] = jnp.dot(ask_s[...], ones, preferred_element_type=F32).astype(BF)
    mine = pl.ds(pl.multiple_of(ctg * 16, 16), 16)
    ask_r[mine, :] = ask_s[mine, :]
    pl.semaphore_wait(barrier, 22)
    asks = []
    for s in range(1, 16):
        p = lax.rem(ctg + s, 16)
        theirs = pl.ds(pl.multiple_of(p * 16, 16), 16)
        asks.append(send(ask_s.at[theirs, :], ask_r.at[mine, :], (p, line)))

    loads["base"].wait()
    base_b[0:112, :] = base_v[0:112, :].astype(BF)
    tail = jnp.concatenate([base_v[112:120, :], jnp.zeros((8, Q), F32)], axis=0)
    base_b[112:128, :] = tail.astype(BF)

    for a in asks:
        a.wait_recv()
    lane = lax.broadcasted_iota(jnp.int32, (256, 128), 1)
    pick = jnp.where(ask_r[...].astype(jnp.int32) == lane, 1.0, 0.0).astype(BF)
    val_s[...] = jnp.dot(pick, base_b[...], preferred_element_type=F32).astype(BF)
    vals = []
    for s in range(1, 16):
        p = lax.rem(ctg + s, 16)
        theirs = pl.ds(pl.multiple_of(p * 16, 16), 16)
        vals.append(send(val_s.at[theirs, :], slots.at[0, mine, :], (p, line)))
    slots[0, mine, :] = val_s[mine, :]

    loads["slot"].wait()
    sl = slot_v[...]
    o = lax.shift_right_logical(sl * 4370, 16)
    j = sl - o * 15
    lo = o & 7
    rel = (lax.shift_right_logical(lo, 1) - z + 4) & 3
    other = (lo & 1) ^ core
    place = (rel * 2 + other) * 256 + lax.shift_right_logical(o, 3) * 16 + j
    loads["lodf"].wait()
    loads["dual"].wait()

    def weigh(i, _):
        rows = pl.ds(pl.multiple_of(i * 32, 32), 32)
        w_v[rows, 0:ML] = (dual_v[rows, :].astype(F32) * lodf_v[rows, :].astype(F32)).astype(BF)
        w_v[rows, ML:MP] = jnp.zeros((32, MP - ML), BF)
        return 0

    lax.fori_loop(0, KD // 32, weigh, 0)
    loads["sens"].wait()
    sens_v[ML:MP, :] = jnp.zeros((MP - ML, 128), BF)
    loads["rating"].wait()

    for v in vals:
        v.wait_recv()

    up, down, sib = device(dz=1), device(dz=-1), device(sibling=True)
    a_up = send(slots.at[0], slots.at[6], up)
    a_down = send(slots.at[0], slots.at[2], down)
    a_sib = send(slots.at[0], slots.at[1], sib)

    row256 = lax.broadcasted_iota(jnp.int32, (256, KD), 0)

    def collect(block, first=False):
        hot = jnp.where(row256 == place - block * 256, 1.0, 0.0).astype(BF)
        part = lax.dot_general(slots[block], hot, (((0,), (0,)), ((), ())), preferred_element_type=F32)
        of_acc[...] = part if first else of_acc[...] + part

    collect(0, first=True)
    a_up.wait_recv()
    f_up = send(slots.at[6, 0:128], slots.at[4, 0:128], up)
    g6 = send(slots.at[6], slots.at[7], sib)
    a_down.wait_recv()
    f_down = send(slots.at[2, 128:256], slots.at[4, 128:256], down)
    g2 = send(slots.at[2], slots.at[3], sib)
    a_sib.wait_recv()
    collect(1)
    collect(6)
    collect(2)
    g6.wait_recv()
    collect(7)
    g2.wait_recv()
    collect(3)
    f_up.wait_recv()
    g4a = send(slots.at[4, 0:128], slots.at[5, 0:128], sib)
    f_down.wait_recv()
    g4b = send(slots.at[4, 128:256], slots.at[5, 128:256], sib)
    collect(4)
    g4a.wait_recv()
    g4b.wait_recv()
    collect(5)
    of_b[...] = of_acc[...].astype(BF)

    def product(h, d, i):
        a, b = (i, d) if h == 0 else (d, i)
        t = mod4(y + a) * 4 + mod4(x + b)
        cols = pl.ds(pl.multiple_of(t * 128, 128), 128)
        return jnp.dot(of_b[h * QH : (h + 1) * QH, :], w_v[:, cols], preferred_element_type=F32)

    def products(h, d):
        def step(i, _):
            s1[h, d, i] = product(h, d, i).astype(BF)
            return 0

        lax.fori_loop(0, 4, step, 0)

    def along(h, stage, d):
        return device(dx=d) if h == stage else device(dy=d)

    opp = [None, None]
    direct = [None, None]
    for h in range(2):
        products(h, 2)
        opp[h] = (send(s1.at[h, 2, 0:2], ro1.at[h, 0], along(h, 0, 1)),
                  send(s1.at[h, 2, 2:4], ro1.at[h, 1], along(h, 0, -1)))
    for h in range(2):
        products(h, 1)
        products(h, 3)
        direct[h] = (send(s1.at[h, 1, 2:4], r1.at[h, 0, 2:4], along(h, 0, 1)),
                     send(s1.at[h, 3, 0:2], r1.at[h, 1, 0:2], along(h, 0, -1)))
    merged = [None, None]
    for h in range(2):
        opp[h][0].wait_recv()
        s1[h, 1, 0:2] = (s1[h, 1, 0:2].astype(F32) + ro1[h, 0].astype(F32)).astype(BF)
        m0 = send(s1.at[h, 1, 0:2], r1.at[h, 0, 0:2], along(h, 0, 1))
        opp[h][1].wait_recv()
        s1[h, 3, 2:4] = (s1[h, 3, 2:4].astype(F32) + ro1[h, 1].astype(F32)).astype(BF)
        m1 = send(s1.at[h, 3, 2:4], r1.at[h, 1, 2:4], along(h, 0, -1))
        merged[h] = (m0, m1)
    for h in range(2):
        def own(i, _):
            own1[h, i] = product(h, 0, i)
            return 0

        lax.fori_loop(0, 4, own, 0)
    HH = QH // 2
    opp2 = [None, None]
    direct2 = [None, None]
    for h in range(2):
        for c in direct[h] + merged[h]:
            c.wait_recv()
        for i in (2, 1, 3):
            s2[h, i] = (own1[h, i] + r1[h, 0, i].astype(F32) + r1[h, 1, i].astype(F32)).astype(BF)
            if i == 2:
                opp2[h] = (send(s2.at[h, 2, 0:HH], ro2.at[h, 0], along(h, 1, 1)),
                           send(s2.at[h, 2, HH:QH], ro2.at[h, 1], along(h, 1, -1)))
        direct2[h] = (send(s2.at[h, 1, HH:QH], r2.at[h, 0, HH:QH], along(h, 1, 1)),
                      send(s2.at[h, 3, 0:HH], r2.at[h, 1, 0:HH], along(h, 1, -1)))
    merged2 = [None, None]
    for h in range(2):
        opp2[h][0].wait_recv()
        s2[h, 1, 0:HH] = (s2[h, 1, 0:HH].astype(F32) + ro2[h, 0].astype(F32)).astype(BF)
        m0 = send(s2.at[h, 1, 0:HH], r2.at[h, 0, 0:HH], along(h, 1, 1))
        opp2[h][1].wait_recv()
        s2[h, 3, HH:QH] = (s2[h, 3, HH:QH].astype(F32) + ro2[h, 1].astype(F32)).astype(BF)
        m1 = send(s2.at[h, 3, HH:QH], r2.at[h, 1, HH:QH], along(h, 1, -1))
        merged2[h] = (m0, m1)

    rows_r = lax.broadcasted_iota(jnp.int32, (16, 128), 0)
    limit = jnp.sum(jnp.where((rows_r == ctg) & (rows_r < 15), rating_v[...], 0.0), axis=0, keepdims=True)
    near1 = [None, None]
    near2 = [{}, {}]
    for h in range(2):
        for c in direct2[h] + merged2[h]:
            c.wait_recv()
        total = own1[h, 0] + own_sum(r1, h) + r2[h, 0].astype(F32) + r2[h, 1].astype(F32)
        ex[h, 0, 0] = (total - jnp.clip(total, -limit, limit)).astype(BF)
        near1[h] = (send(ex.at[h, 0, 0], ex.at[h, 0, 3], along(h, 1, 1)),
                    send(ex.at[h, 0, 0], ex.at[h, 0, 1], along(h, 1, -1)))

    def spread(h, i):
        near2[h][i] = (send(ex.at[h, 0, i], ex.at[h, 3, i], along(h, 0, 1)),
                       send(ex.at[h, 0, i], ex.at[h, 1, i], along(h, 0, -1)))

    def absorb(h, d, i, first=False):
        a, b = (i, d) if h == 0 else (d, i)
        t = mod4(y + a) * 4 + mod4(x + b)
        rows = pl.ds(pl.multiple_of(t * 128, 128), 128)
        part = jnp.dot(ex[h, d, i], sens_v[rows, :], preferred_element_type=F32)
        cut_acc[h] = part if first else cut_acc[h] + part

    far1 = [None, None]
    far2 = [{}, {}]
    for h in range(2):
        spread(h, 0)
        absorb(h, 0, 0, first=True)
    for h in range(2):
        near1[h][0].wait_recv()
        f0 = send(ex.at[h, 0, 3, 0:HH], ex.at[h, 0, 2, 0:HH], along(h, 1, 1))
        near1[h][1].wait_recv()
        f1 = send(ex.at[h, 0, 1, HH:QH], ex.at[h, 0, 2, HH:QH], along(h, 1, -1))
        far1[h] = (f0, f1)
        spread(h, 3)
        spread(h, 1)
        absorb(h, 0, 3)
        absorb(h, 0, 1)
    def pass_on(h, i):
        near2[h][i][0].wait_recv()
        if i < 2:
            far2[h][i] = send(ex.at[h, 3, i], ex.at[h, 2, i], along(h, 0, 1))
        near2[h][i][1].wait_recv()
        if i >= 2:
            far2[h][i] = send(ex.at[h, 1, i], ex.at[h, 2, i], along(h, 0, -1))
        absorb(h, 3, i)
        absorb(h, 1, i)

    for h in range(2):
        pass_on(h, 0)
    for h in range(2):
        far1[h][0].wait_recv()
        far1[h][1].wait_recv()
        spread(h, 2)
        absorb(h, 0, 2)
    for i in (1, 3, 2):
        for h in range(2):
            pass_on(h, i)
    for i in (0, 1, 3, 2):
        for h in range(2):
            far2[h][i].wait_recv()
            absorb(h, 2, i)

    for h in range(2):
        cut_v[h * QH : (h + 1) * QH, :] = cut_acc[h]
    flipped = [cut_v[i * 128 : (i + 1) * 128, :].T for i in range(3)]
    for i in range(3):
        cut_t = flipped[i]
        for p in range(8):
            fin_r[8 + p, :, i * 128 : (i + 1) * 128] = cut_t[p * 16 : (p + 1) * 16, :]
    fins = []
    for s in range(1, 8):
        p = lax.rem(line + s, 8)
        fins.append(send(fin_r.at[8 + p], fin_r.at[s], (ctg, p)))
    total = fin_r[8 + line]
    for s, f in enumerate(fins):
        f.wait_recv()
        total = total + fin_r[s + 1]
    out_ref[...] = total
    for c in sent:
        c.wait_send()


def own_sum(r1, h):
    return r1[h, 0, 0].astype(F32) + r1[h, 1, 0].astype(F32)


def per_device(base_flow, lodf, dual, rating, sens, fetch_rows, ctg_slot):
    hbm = pl.BlockSpec(memory_space=pl.ANY)
    vm = pltpu.VMEM
    return pl.pallas_call(
        kernel,
        out_shape=jax.ShapeDtypeStruct((16, Q), F32),
        in_specs=[hbm] * 7,
        out_specs=pl.BlockSpec(memory_space=pltpu.VMEM),
        scratch_shapes=[
            vm((16, 128), jnp.int32), vm((1, KD), jnp.int32), vm((120, Q), F32), vm((128, Q), BF),
            vm((KD, ML), BF), vm((KD, ML), BF), vm((16, 128), F32), vm((MP, 128), BF), vm((KD, MP), BF),
            vm((256, 128), BF), vm((256, 128), BF), vm((256, Q), BF), vm((8, 256, Q), BF),
            vm((Q, KD), F32), vm((Q, KD), BF),
            vm((2, 4, 4, QH, 128), BF), vm((2, 4, QH, 128), F32), vm((2, 2, 2, QH, 128), BF), vm((2, 2, 4, QH, 128), BF),
            vm((2, 4, QH, 128), BF), vm((2, 2, QH // 2, 128), BF), vm((2, 2, QH, 128), BF),
            vm((2, 4, 4, QH, 128), BF), vm((2, QH, 128), F32), vm((Q, 128), F32), vm((16, 16, Q), F32),
            pltpu.SemaphoreType.DMA((8,)), pltpu.SemaphoreType.DMA((N_SEM,)), pltpu.SemaphoreType.DMA((N_SEM,)),
        ],
        compiler_params=pltpu.CompilerParams(
            collective_id=0, has_side_effects=True, vmem_limit_bytes=56 * 1024 * 1024
        ),
    )(fetch_rows[0].T, ctg_slot[None, :], base_flow.T, lodf.T, dual.T, rating.reshape(15, 128), sens)


def solution(mesh):
    in_specs = (
        P(None, ("ctg", "line")),
        P("line", "ctg"),
        P("line", "ctg"),
        P("line"),
        P("line", "ctg"),
        P("ctg", None, None),
        P("ctg"),
    )
    out_specs = P(("ctg", "line"), None)
    return jax.shard_map(
        per_device, mesh=mesh, in_specs=in_specs, out_specs=out_specs, check_vma=False
    )
```

```python
import jax
import jax.numpy as jnp
from jax import lax
from jax.experimental import pallas as pl
from jax.experimental.pallas import tpu as pltpu
from jax.sharding import PartitionSpec as P

MESH = pl.DeviceIdType.MESH
BF = jnp.bfloat16
F32 = jnp.float32
Q = 384
NC = 3
HR = 64
KD = 960
ML = 1920
MP = 2048
N_SEM = 144


def mod4(v):
    return lax.rem(v + 4, 4)


def at128(i):
    return pl.ds(pl.multiple_of(i * 128, 128), 128)


def kernel(
    fr_h, slot_h, base_h, lodf_h, dual_h, rating_h, sens_h, out_ref,
    fr_v, slot_v, base_v, base_b, lodf_v, dual_v, rating_v, sens_v, sens_x, w_v, hot,
    ask_s, ask_r, val_s, slots, of_b,
    s1, r1, t2, s2, r2, ex, part, kr, u_v, zs, zr, v_v, rr,
    load_sem, send_sem, recv_sem,
):
    ctg = lax.axis_index("ctg")
    line = lax.axis_index("line")
    y, x = lax.div(ctg, 4), lax.rem(ctg, 4)
    z, core = lax.div(line, 2), lax.rem(line, 2)
    here = (x, y)
    sent = []

    def send(src, dst, to):
        i = len(sent)
        copy = pltpu.make_async_remote_copy(
            src_ref=src, dst_ref=dst, send_sem=send_sem.at[i], recv_sem=recv_sem.at[i],
            device_id=to, device_id_type=MESH,
        )
        sent.append(copy)
        copy.start()
        return copy

    def along(axis, d):
        return (y * 4 + mod4(x + d), line) if axis == 0 else (mod4(y + d) * 4 + x, line)

    sib = (ctg, z * 2 + 1 - core)

    loads = {}
    plan = [("fr", fr_h, fr_v.at[0:15]), ("base", base_h, base_v), ("slot", slot_h, slot_v),
            ("lodf", lodf_h, lodf_v), ("dual", dual_h, dual_v),
            ("sens0", sens_h.at[0:4], sens_v.at[0]), ("sens1", sens_h.at[4:8], sens_v.at[1]),
            ("sens2", sens_h.at[8:12], sens_v.at[2]), ("sens3", sens_h.at[12:15], sens_v.at[3, 0:3]),
            ("rating", rating_h, rating_v.at[0:15])]
    for i, (name, src, dst) in enumerate(plan):
        loads[name] = pltpu.make_async_copy(src, dst, load_sem.at[i])
        loads[name].start()

    barrier = pltpu.get_barrier_semaphore()
    for s in range(1, 16):
        pl.semaphore_signal(barrier, inc=1, device_id=(lax.rem(ctg + s, 16), line), device_id_type=MESH)
    for e in range(1, 4):
        pl.semaphore_signal(barrier, inc=1, device_id=(ctg, mod4(z + e) * 2 + core), device_id_type=MESH)
    pl.semaphore_signal(barrier, inc=1, device_id=sib, device_id_type=MESH)

    loads["fr"].wait()
    row16 = lax.broadcasted_iota(jnp.int32, (16, 128), 0)
    lane16 = lax.broadcasted_iota(jnp.int32, (16, 128), 1)
    fr_v[15] = jnp.full((1, 128), -1, jnp.int32)
    table = fr_v[...].reshape(16, 128).astype(F32)
    ones = jnp.ones((128, 128), BF)
    for c in range(16):
        ask_s[c * 16 : c * 16 + 16, :] = jnp.where(lane16 == c * 8 + line, table, 0.0).astype(BF)
    ask_s[...] = jnp.dot(ask_s[...], ones, preferred_element_type=F32).astype(BF)
    mine = pl.ds(pl.multiple_of(ctg * 16, 16), 16)
    ask_r[mine, :] = ask_s[mine, :]
    pl.semaphore_wait(barrier, 19)
    asks = []
    for s in range(1, 16):
        p = lax.rem(ctg + s, 16)
        theirs = pl.ds(pl.multiple_of(p * 16, 16), 16)
        asks.append(send(ask_s.at[theirs, :], ask_r.at[mine, :], (p, line)))

    loads["base"].wait()
    base_b[0:112, :] = base_v[0:112, :].astype(BF)
    tail = jnp.concatenate([base_v[112:120, :], jnp.zeros((8, Q), F32)], axis=0)
    base_b[112:128, :] = tail.astype(BF)
    loads["slot"].wait()
    sl = slot_v[...]
    o = lax.shift_right_logical(sl * 4370, 16)
    lo = o & 7
    rel = (z - lax.shift_right_logical(lo, 1) + 4) & 3
    other = (lo & 1) ^ core
    place = (other * 4 + rel) * 256 + lax.shift_right_logical(o, 3) * 16 + (sl - o * 15)
    row256 = lax.broadcasted_iota(jnp.int32, (256, KD), 0)

    def heat(b, _):
        hot[pl.ds(pl.multiple_of(b * 256, 256), 256), :] = jnp.where(row256 == place - b * 256, 1.0, 0.0).astype(BF)
        return 0

    lax.fori_loop(0, 8, heat, 0)

    for a in asks:
        a.wait_recv()
    lane = lax.broadcasted_iota(jnp.int32, (256, 128), 1)
    pick = jnp.where(ask_r[...].astype(jnp.int32) == lane, 1.0, 0.0).astype(BF)
    found = jnp.dot(pick, base_b[...], preferred_element_type=F32).astype(BF)
    for i in range(NC):
        val_s[i] = found[:, i * 128 : (i + 1) * 128]
    vals = []
    for s in range(1, 16):
        p = lax.rem(ctg + s, 16)
        theirs = pl.ds(pl.multiple_of(p * 16, 16), 16)
        vals.append(send(val_s.at[:, theirs, :], slots.at[:, 0, mine, :], (p, line)))
    for i in range(NC):
        slots[i, 0, mine, :] = val_s[i, mine, :]

    for name in ("sens0", "sens1", "sens2", "sens3"):
        loads[name].wait()
    sens_v[3, 3] = jnp.zeros((128, 128), BF)
    sens_x[0, :, :, 0:128] = sens_v[y]
    sens_x[1, :, :, 0:128] = sens_v[:, x]
    loads["lodf"].wait()
    loads["dual"].wait()

    def weigh(i, _):
        rows = pl.ds(pl.multiple_of(i * 32, 32), 32)
        w_v[rows, 0:ML] = (dual_v[rows, :].astype(F32) * lodf_v[rows, :].astype(F32)).astype(BF)
        w_v[rows, ML:MP] = jnp.zeros((32, MP - ML), BF)
        return 0

    lax.fori_loop(0, KD // 32, weigh, 0)
    loads["rating"].wait()
    rows_r = lax.broadcasted_iota(jnp.int32, (16, 128), 0)
    limit = jnp.sum(jnp.where((rows_r == ctg) & (rows_r < 15), rating_v[...], 0.0), axis=0, keepdims=True)

    for v in vals:
        v.wait_recv()

    far, near, relayed = [None] * NC, [None] * NC, [None] * NC

    def gather(i):
        far[i] = [send(slots.at[i, 0], slots.at[i, e], (ctg, mod4(z + e) * 2 + core)) for e in (2, 1, 3)]
        near[i] = send(slots.at[i, 0], slots.at[i, 4], sib)

    def relay(i):
        for c in far[i]:
            c.wait_recv()
        relayed[i] = send(slots.at[i, 1:4], slots.at[i, 5:8], sib)

    def collect(i):
        tn = (((0,), (0,)), ((), ()))
        a = lax.dot_general(slots[i, 0:4].reshape(1024, 128), hot[0:1024, :], tn, preferred_element_type=F32)
        near[i].wait_recv()
        relayed[i].wait_recv()
        b = lax.dot_general(slots[i, 4:8].reshape(1024, 128), hot[1024:2048, :], tn, preferred_element_type=F32)
        of_b[i] = (a + b).astype(BF)

    sum1, sum2 = [[[], []] for _ in range(NC)], [[[], []] for _ in range(NC)]

    def shifts(i):
        for e in (2, 1, 3, 0):
            g = mod4(y + e)
            cols = pl.ds(pl.multiple_of(g * 512, 512), 512)
            got = jnp.dot(of_b[i], w_v[:, cols], preferred_element_type=F32).astype(BF)
            for t in range(4):
                tile = got[:, t * 128 : (t + 1) * 128]
                s1[i, 0, t, g] = tile[0:HR]
                s1[i, 1, g, t] = tile[HR:128]
            if e:
                sum1[i][1].append(send(s1.at[i, 1, g], r1.at[i, 1, e - 1], along(1, e)))
        for e in (2, 1, 3):
            sum1[i][0].append(send(s1.at[i, 0, mod4(x + e)], r1.at[i, 0, e - 1], along(0, e)))

    def second(i):
        for h in (1, 0):
            for c in sum1[i][h]:
                c.wait_recv()
            total = s1[i, h, here[h]].astype(F32)
            for e in range(3):
                total = total + r1[i, h, e].astype(F32)
            t2[i, h] = total
            s2[i, h] = total.astype(BF)
            for e in (2, 1, 3):
                sum2[i][h].append(
                    send(s2.at[i, h, mod4(here[1 - h] + e)], r2.at[i, h, e - 1], along(1 - h, e)))

    gathered = [[[], []] for _ in range(NC)]

    def excess(i):
        for h in (1, 0):
            for c in sum2[i][h]:
                c.wait_recv()
            total = t2[i, h, here[1 - h]]
            for e in range(3):
                total = total + r2[i, h, e].astype(F32)
            lanes = at128(here[h])
            ex[i, h, :, lanes] = (total - jnp.clip(total, -limit, limit)).astype(BF)
            for e in (2, 1, 3):
                gathered[i][h].append(send(ex.at[i, h, :, lanes], ex.at[i, h, :, lanes], along(h, e)))

    crossed, zsum, last = [None] * NC, [None] * NC, [[] for _ in range(NC)]

    def cut(i):
        both = []
        for h in range(2):
            for c in gathered[i][h]:
                c.wait_recv()
            both.append(jnp.dot(ex[i, h], sens_x[h].reshape(512, 512), preferred_element_type=F32))
        both = jnp.concatenate(both, axis=0)
        for e in range(4):
            part[i, e] = both[:, e * 128 : (e + 1) * 128].T.reshape(4, 2, 16, 128)
        crossed[i] = send(part.at[i, :, :, 1 - core], kr.at[i], sib)

    def cut_z(i):
        crossed[i].wait_recv()
        total = part[i, :, :, core] + kr[i]
        u_v[i] = total
        zs[i] = total.astype(BF)
        zsum[i] = [send(zs.at[i, :, mod4(z + e)], zr.at[i, e - 1], (ctg, mod4(z + e) * 2 + core)) for e in (2, 1, 3)]

    def cut_last(i):
        for c in zsum[i]:
            c.wait_recv()
        total = u_v[i, :, z]
        for e in range(3):
            total = total + zr[i, e].astype(F32)
        v_v[i] = total
        for h in range(2):
            for e in (2, 1, 3):
                last[i].append(send(v_v.at[i, e], rr.at[i, h, e - 1], along(1 - h, -e)))

    def finish(i):
        for c in last[i]:
            c.wait_recv()
        lane_o = lax.broadcasted_iota(jnp.int32, (16, 128), 1)
        total = v_v[i, 0]
        for e in range(3):
            total = total + jnp.where(lane_o < HR, rr[i, 0, e], rr[i, 1, e])
        out_ref[:, i * 128 : (i + 1) * 128] = total

    for i in range(NC):
        gather(i)
    swaps = []
    for e in (2, 1, 3):
        swaps.append(send(sens_v.at[mod4(y + e)], sens_x.at[0, :, :, e * 128 : (e + 1) * 128], along(1, e)))
        swaps.append(send(sens_v.at[:, mod4(x + e)], sens_x.at[1, :, :, e * 128 : (e + 1) * 128], along(0, e)))
    relay(0)
    collect(0)
    shifts(0)
    relay(1)
    collect(1)
    shifts(1)
    relay(2)
    collect(2)
    second(0)
    shifts(2)
    second(1)
    excess(0)
    for c in swaps:
        c.wait_recv()
    second(2)
    excess(1)
    cut(0)
    excess(2)
    cut_z(0)
    cut(1)
    cut_z(1)
    cut_last(0)
    cut(2)
    cut_last(1)
    cut_z(2)
    cut_last(2)
    for i in range(NC):
        finish(i)
    for c in sent:
        c.wait_send()


def per_device(base_flow, lodf, dual, rating, sens, fetch_rows, ctg_slot):
    hbm = pl.BlockSpec(memory_space=pl.ANY)
    vm = pltpu.VMEM
    return pl.pallas_call(
        kernel,
        out_shape=jax.ShapeDtypeStruct((16, Q), F32),
        in_specs=[hbm] * 7,
        out_specs=pl.BlockSpec(memory_space=pltpu.VMEM),
        scratch_shapes=[
            vm((16, 1, 128), jnp.int32), vm((1, KD), jnp.int32), vm((120, Q), F32), vm((128, Q), BF),
            vm((KD, ML), BF), vm((KD, ML), BF), vm((16, 128), F32), vm((4, 4, 128, 128), BF), vm((2, 4, 128, 512), BF),
            vm((KD, MP), BF), vm((2048, KD), BF),
            vm((256, 128), BF), vm((256, 128), BF), vm((NC, 256, 128), BF), vm((NC, 8, 256, 128), BF), vm((NC, 128, KD), BF),
            vm((NC, 2, 4, 4, HR, 128), BF), vm((NC, 2, 3, 4, HR, 128), BF), vm((NC, 2, 4, HR, 128), F32),
            vm((NC, 2, 4, HR, 128), BF), vm((NC, 2, 3, HR, 128), BF), vm((NC, 2, HR, 512), BF),
            vm((NC, 4, 4, 2, 16, 128), F32), vm((NC, 4, 4, 16, 128), F32), vm((NC, 4, 4, 16, 128), F32),
            vm((NC, 4, 4, 16, 128), BF), vm((NC, 3, 4, 16, 128), BF), vm((NC, 4, 16, 128), F32), vm((NC, 2, 3, 16, 128), F32),
            pltpu.SemaphoreType.DMA((10,)), pltpu.SemaphoreType.DMA((N_SEM,)), pltpu.SemaphoreType.DMA((N_SEM,)),
        ],
        compiler_params=pltpu.CompilerParams(
            collective_id=0, has_side_effects=True, vmem_limit_bytes=56 * 1024 * 1024
        ),
    )(fetch_rows.transpose(2, 0, 1), ctg_slot[None, :], base_flow.T, lodf.T, dual.T, rating.reshape(15, 128),
      sens.reshape(15, 128, 128))


def solution(mesh):
    in_specs = (
        P(None, ("ctg", "line")),
        P("line", "ctg"),
        P("line", "ctg"),
        P("line"),
        P("line", "ctg"),
        P("ctg", None, None),
        P("ctg"),
    )
    out_specs = P(("ctg", "line"), None)
    return jax.shard_map(
        per_device, mesh=mesh, in_specs=in_specs, out_specs=out_specs, check_vma=False
    )
```

```python
import jax
import jax.numpy as jnp
from jax import lax
from jax.experimental import pallas as pl
from jax.experimental.pallas import tpu as pltpu
from jax.sharding import PartitionSpec as P

MESH = pl.DeviceIdType.MESH
BF = jnp.bfloat16
F32 = jnp.float32
Q = 384
NC = 3
HR = 64
KD = 960
ML = 1920
MP = 2048
N_SEM = 160


def mod4(v):
    return lax.rem(v + 4, 4)


def at128(i):
    return pl.ds(pl.multiple_of(i * 128, 128), 128)


def kernel(
    fr_h, slot_h, base_h, lodf_h, dual_h, rating_h, sens_h, out_ref,
    slot_v, base_v, base_b, lodf_v, dual_v, rating_v, sens_v, sens_x, w_v, hot,
    ask_r, val_s, slots, of_b,
    s1, r1, t2, s2, r2, ex, part, zs, zr, v_v, rr,
    load_sem, send_sem, recv_sem,
):
    ctg = lax.axis_index("ctg")
    line = lax.axis_index("line")
    y, x = lax.div(ctg, 4), lax.rem(ctg, 4)
    z, core = lax.div(line, 2), lax.rem(line, 2)
    here = (x, y)
    sent, ended = [], set()

    def send(src, dst, to):
        i = len(sent)
        copy = pltpu.make_async_remote_copy(
            src_ref=src, dst_ref=dst, send_sem=send_sem.at[i], recv_sem=recv_sem.at[i],
            device_id=to, device_id_type=MESH,
        )
        sent.append(copy)
        copy.start()
        return copy

    def drain(copies):
        for c in copies:
            if id(c) not in ended:
                c.wait_send()
                ended.add(id(c))

    def along(axis, d):
        return (y * 4 + mod4(x + d), line) if axis == 0 else (mod4(y + d) * 4 + x, line)

    sib = (ctg, z * 2 + 1 - core)
    steps = sorted(((a, b) for a in range(4) for b in range(4) if a or b), key=lambda ab: -(min(ab[0], 4 - ab[0]) + min(ab[1], 4 - ab[1])))
    peers = [mod4(y + a) * 4 + mod4(x + b) for a, b in steps]

    loads = {}
    plan = [("base", base_h, base_v), ("slot", slot_h, slot_v),
            ("lodf", lodf_h, lodf_v), ("dual", dual_h, dual_v),
            ("sens0", sens_h.at[0:4], sens_v.at[0]), ("sens1", sens_h.at[4:8], sens_v.at[1]),
            ("sens2", sens_h.at[8:12], sens_v.at[2]), ("sens3", sens_h.at[12:15], sens_v.at[3, 0:3]),
            ("rating", rating_h, rating_v.at[0:15])]
    for i, (name, src, dst) in enumerate(plan):
        loads[name] = pltpu.make_async_copy(src, dst, load_sem.at[i + 1])
        loads[name].start()

    barrier = pltpu.get_barrier_semaphore()
    for p in peers:
        pl.semaphore_signal(barrier, inc=1, device_id=(p, line), device_id_type=MESH)
    for e in range(1, 8):
        pl.semaphore_signal(barrier, inc=1, device_id=(ctg, lax.rem(line + e, 8)), device_id_type=MESH)

    mine = pl.ds(pl.multiple_of(ctg * 16, 16), 16)
    pl.semaphore_wait(barrier, 22)
    asks = [send(fr_h, ask_r.at[ctg, 0:15], (p, line)) for p in peers]
    own_ask = pltpu.make_async_copy(fr_h, ask_r.at[ctg, 0:15], load_sem.at[0])
    own_ask.start()
    ask_r[:, 15:16] = jnp.full((16, 1, 1, 128), -1, jnp.int32)

    loads["base"].wait()
    base_b[0:112, :] = base_v[0:112, :].astype(BF)
    tail = jnp.concatenate([base_v[112:120, :], jnp.zeros((8, Q), F32)], axis=0)
    base_b[112:128, :] = tail.astype(BF)
    loads["slot"].wait()
    sl = slot_v[...]
    o = lax.shift_right_logical(sl * 4370, 16)
    lo = o & 7
    rel = (z - lax.shift_right_logical(lo, 1) + 4) & 3
    other = (lo & 1) ^ core
    place = (other * 4 + rel) * 256 + lax.shift_right_logical(o, 3) * 16 + (sl - o * 15)
    row256 = lax.broadcasted_iota(jnp.int32, (256, KD), 0)

    def heat(b, _):
        hot[pl.ds(pl.multiple_of(b * 256, 256), 256), :] = jnp.where(row256 == place - b * 256, 1.0, 0.0).astype(BF)
        return 0

    lax.fori_loop(0, 8, heat, 0)

    for a in asks:
        a.wait_recv()
    own_ask.wait()
    lane = lax.broadcasted_iota(jnp.int32, (256, 128), 1)
    wanted = jnp.where(lane == ctg * 8 + line, ask_r[...].reshape(256, 128), 0).astype(BF)
    wanted = jnp.dot(wanted, jnp.ones((128, 128), BF), preferred_element_type=F32)
    pick = jnp.where(wanted == lane.astype(F32), 1.0, 0.0).astype(BF)
    found = jnp.dot(pick, base_b[...], preferred_element_type=F32).astype(BF)
    for i in range(NC):
        val_s[i] = found[:, i * 128 : (i + 1) * 128]
    vals = []
    for p in peers:
        theirs = pl.ds(pl.multiple_of(p * 16, 16), 16)
        vals.append(send(val_s.at[:, theirs, :], slots.at[:, 0, mine, :], (p, line)))
    for i in range(NC):
        slots[i, 0, mine, :] = val_s[i, mine, :]

    for name in ("sens0", "sens1", "sens2", "sens3"):
        loads[name].wait()
    sens_v[3, 3] = jnp.zeros((128, 128), BF)
    sens_x[0, :, :, 0:128] = sens_v[y]
    sens_x[1, :, :, 0:128] = sens_v[:, x]
    loads["lodf"].wait()
    loads["dual"].wait()

    def weigh(i, _):
        rows = pl.ds(pl.multiple_of(i * 32, 32), 32)
        w_v[rows, 0:ML] = (dual_v[rows, :].astype(F32) * lodf_v[rows, :].astype(F32)).astype(BF)
        w_v[rows, ML:MP] = jnp.zeros((32, MP - ML), BF)
        return 0

    lax.fori_loop(0, KD // 32, weigh, 0)
    loads["rating"].wait()
    rows_r = lax.broadcasted_iota(jnp.int32, (16, 128), 0)
    limit = jnp.sum(jnp.where((rows_r == ctg) & (rows_r < 15), rating_v[...], 0.0), axis=0, keepdims=True)

    for v in vals:
        v.wait_recv()

    far, near, relayed = [None] * NC, [None] * NC, [None] * NC

    def gather(i):
        far[i] = [send(slots.at[i, 0], slots.at[i, e], (ctg, mod4(z + e) * 2 + core)) for e in (2, 1, 3)]
        near[i] = send(slots.at[i, 0], slots.at[i, 4], sib)

    def relay(i):
        for c in far[i]:
            c.wait_recv()
        relayed[i] = send(slots.at[i, 1:4], slots.at[i, 5:8], sib)

    def collect(i):
        tn = (((0,), (0,)), ((), ()))
        a = lax.dot_general(slots[i, 0:4].reshape(1024, 128), hot[0:1024, :], tn, preferred_element_type=F32)
        near[i].wait_recv()
        relayed[i].wait_recv()
        b = lax.dot_general(slots[i, 4:8].reshape(1024, 128), hot[1024:2048, :], tn, preferred_element_type=F32)
        of_b[i] = (a + b).astype(BF)

    sum1, sum2 = [[[], []] for _ in range(NC)], [[[], []] for _ in range(NC)]

    def shifts(i):
        for e in (2, 1, 3, 0):
            g = mod4(y + e)
            cols = pl.ds(pl.multiple_of(g * 512, 512), 512)
            got = jnp.dot(of_b[i], w_v[:, cols], preferred_element_type=F32).astype(BF)
            for t in range(4):
                tile = got[:, t * 128 : (t + 1) * 128]
                s1[i, 0, t, g] = tile[0:HR]
                s1[i, 1, g, t] = tile[HR:128]
            if e:
                sum1[i][1].append(send(s1.at[i, 1, g], r1.at[i, 1, e - 1], along(1, e)))
        for e in (2, 1, 3):
            sum1[i][0].append(send(s1.at[i, 0, mod4(x + e)], r1.at[i, 0, e - 1], along(0, e)))

    def second(i):
        for h in (1, 0):
            for c in sum1[i][h]:
                c.wait_recv()
            total = s1[i, h, here[h]].astype(F32)
            for e in range(3):
                total = total + r1[i, h, e].astype(F32)
            t2[i, h] = total
            s2[i, h] = total.astype(BF)
            for e in (2, 1, 3):
                sum2[i][h].append(
                    send(s2.at[i, h, mod4(here[1 - h] + e)], r2.at[i, h, e - 1], along(1 - h, e)))

    gathered = [[[], []] for _ in range(NC)]

    def excess(i):
        for h in (1, 0):
            for c in sum2[i][h]:
                c.wait_recv()
            total = t2[i, h, here[1 - h]]
            for e in range(3):
                total = total + r2[i, h, e].astype(F32)
            lanes = at128(here[h])
            ex[i, h, :, lanes] = (total - jnp.clip(total, -limit, limit)).astype(BF)
            for e in (2, 1, 3):
                gathered[i][h].append(send(ex.at[i, h, :, lanes], ex.at[i, h, :, lanes], along(h, e)))

    zsum, last = [None] * NC, [[] for _ in range(NC)]

    def cut(i):
        both = []
        for h in range(2):
            for c in gathered[i][h]:
                c.wait_recv()
            both.append(jnp.dot(ex[i, h], sens_x[h].reshape(512, 512), preferred_element_type=F32))
        both = jnp.concatenate(both, axis=0)
        for e in range(4):
            flat = both[:, e * 128 : (e + 1) * 128].T.reshape(8, 16, 128)
            part[i, e] = flat
            zs[i, e] = flat.astype(BF)
        zsum[i] = []
        for e in (4, 5, 3, 2, 6, 7, 1):
            p = lax.rem(line + e, 8)
            zsum[i].append(send(zs.at[i, :, p], zr.at[i, e - 1], (ctg, p)))

    def cut_last(i):
        for c in zsum[i]:
            c.wait_recv()
        total = part[i, :, line]
        for e in range(7):
            total = total + zr[i, e].astype(F32)
        v_v[i] = total
        for h in range(2):
            for e in (2, 1, 3):
                last[i].append(send(v_v.at[i, e], rr.at[i, h, e - 1], along(1 - h, -e)))

    def finish(i):
        for c in last[i]:
            c.wait_recv()
        lane_o = lax.broadcasted_iota(jnp.int32, (16, 128), 1)
        total = v_v[i, 0]
        for e in range(3):
            total = total + jnp.where(lane_o < HR, rr[i, 0, e], rr[i, 1, e])
        out_ref[:, i * 128 : (i + 1) * 128] = total

    for i in range(NC):
        gather(i)
    swaps = []
    for e in (2, 1, 3):
        swaps.append(send(sens_v.at[mod4(y + e)], sens_x.at[0, :, :, e * 128 : (e + 1) * 128], along(1, e)))
        swaps.append(send(sens_v.at[:, mod4(x + e)], sens_x.at[1, :, :, e * 128 : (e + 1) * 128], along(0, e)))
    old = len(sent)
    relay(0)
    collect(0)
    shifts(0)
    for i in range(1, NC):
        relay(i)
        collect(i)
        shifts(i)
    for i in range(NC):
        second(i)
    drain(sent[:old])
    old = len(sent) - 6
    for i in range(NC):
        excess(i)
    for c in swaps:
        c.wait_recv()
    drain(sent[:old])
    for i in range(NC):
        cut(i)
    for i in range(NC):
        cut_last(i)
    for i in range(NC):
        finish(i)
    drain(sent)


def per_device(base_flow, lodf, dual, rating, sens, fetch_rows, ctg_slot):
    hbm = pl.BlockSpec(memory_space=pl.ANY)
    vm = pltpu.VMEM
    return pl.pallas_call(
        kernel,
        out_shape=jax.ShapeDtypeStruct((16, Q), F32),
        in_specs=[hbm] * 7,
        out_specs=pl.BlockSpec(memory_space=pltpu.VMEM),
        scratch_shapes=[
            vm((1, KD), jnp.int32), vm((120, Q), F32), vm((128, Q), BF),
            vm((KD, ML), BF), vm((KD, ML), BF), vm((16, 128), F32), vm((4, 4, 128, 128), BF), vm((2, 4, 128, 512), BF),
            vm((KD, MP), BF), vm((2048, KD), BF),
            vm((16, 16, 1, 128), jnp.int32), vm((NC, 256, 128), BF), vm((NC, 8, 256, 128), BF), vm((NC, 128, KD), BF),
            vm((NC, 2, 4, 4, HR, 128), BF), vm((NC, 2, 3, 4, HR, 128), BF), vm((NC, 2, 4, HR, 128), F32),
            vm((NC, 2, 4, HR, 128), BF), vm((NC, 2, 3, HR, 128), BF), vm((NC, 2, HR, 512), BF),
            vm((NC, 4, 8, 16, 128), F32), vm((NC, 4, 8, 16, 128), BF), vm((NC, 7, 4, 16, 128), BF), vm((NC, 4, 16, 128), F32), vm((NC, 2, 3, 16, 128), F32),
            pltpu.SemaphoreType.DMA((10,)), pltpu.SemaphoreType.DMA((N_SEM,)), pltpu.SemaphoreType.DMA((N_SEM,)),
        ],
        compiler_params=pltpu.CompilerParams(
            collective_id=0, has_side_effects=True, vmem_limit_bytes=56 * 1024 * 1024
        ),
    )(fetch_rows.transpose(2, 0, 1), ctg_slot[None, :], base_flow.T, lodf.T, dual.T, rating.reshape(15, 128),
      sens.reshape(15, 128, 128))


def solution(mesh):
    in_specs = (
        P(None, ("ctg", "line")),
        P("line", "ctg"),
        P("line", "ctg"),
        P("line"),
        P("line", "ctg"),
        P("ctg", None, None),
        P("ctg"),
    )
    out_specs = P(("ctg", "line"), None)
    return jax.shard_map(
        per_device, mesh=mesh, in_specs=in_specs, out_specs=out_specs, check_vma=False
    )
```

```python
import jax
import jax.numpy as jnp
from jax import lax
from jax.experimental import pallas as pl
from jax.experimental.pallas import tpu as pltpu
from jax.sharding import PartitionSpec as P

MESH = pl.DeviceIdType.MESH
BF = jnp.bfloat16
F32 = jnp.float32
Q = 384
NC = 3
HR = 64
KD = 960
ML = 1920
MP = 2048
N_SEM = 160


def mod4(v):
    return lax.rem(v + 4, 4)


def at128(i):
    return pl.ds(pl.multiple_of(i * 128, 128), 128)


def kernel(
    fr_h, slot_h, base_h, lodf_h, dual_h, rating_h, sens_h, out_ref,
    fr_v, slot_v, base_v, base_b, lodf_v, dual_v, rating_v, sens_v, sens_x, w_v, hot,
    ask_s, ask_r, val_s, slots, of_b,
    s1, r1, t2, s2, r2, ex, part, zs, zr, v_v, rr,
    load_sem, send_sem, recv_sem,
):
    ctg = lax.axis_index("ctg")
    line = lax.axis_index("line")
    y, x = lax.div(ctg, 4), lax.rem(ctg, 4)
    z, core = lax.div(line, 2), lax.rem(line, 2)
    here = (x, y)
    sent, ended = [], set()

    def send(src, dst, to):
        i = len(sent)
        copy = pltpu.make_async_remote_copy(
            src_ref=src, dst_ref=dst, send_sem=send_sem.at[i], recv_sem=recv_sem.at[i],
            device_id=to, device_id_type=MESH,
        )
        sent.append(copy)
        copy.start()
        return copy

    def drain(copies):
        for c in copies:
            if id(c) not in ended:
                c.wait_send()
                ended.add(id(c))

    def along(axis, d):
        return (y * 4 + mod4(x + d), line) if axis == 0 else (mod4(y + d) * 4 + x, line)

    sib = (ctg, z * 2 + 1 - core)
    steps = sorted(((a, b) for a in range(4) for b in range(4) if a or b), key=lambda ab: -(min(ab[0], 4 - ab[0]) + min(ab[1], 4 - ab[1])))
    peers = [mod4(y + a) * 4 + mod4(x + b) for a, b in steps]

    loads = {}
    plan = [("fr", fr_h, fr_v.at[0:15]), ("base", base_h, base_v), ("slot", slot_h, slot_v),
            ("lodf", lodf_h, lodf_v), ("dual", dual_h, dual_v),
            ("sens0", sens_h.at[0:4], sens_v.at[0]), ("sens1", sens_h.at[4:8], sens_v.at[1]),
            ("sens2", sens_h.at[8:12], sens_v.at[2]), ("sens3", sens_h.at[12:15], sens_v.at[3, 0:3]),
            ("rating", rating_h, rating_v.at[0:15])]
    for i, (name, src, dst) in enumerate(plan):
        loads[name] = pltpu.make_async_copy(src, dst, load_sem.at[i])
        loads[name].start()

    barrier = pltpu.get_barrier_semaphore()
    for p in peers:
        pl.semaphore_signal(barrier, inc=1, device_id=(p, line), device_id_type=MESH)
    for e in range(1, 8):
        pl.semaphore_signal(barrier, inc=1, device_id=(ctg, lax.rem(line + e, 8)), device_id_type=MESH)

    mine = pl.ds(pl.multiple_of(ctg * 16, 16), 16)
    loads["fr"].wait()
    fr_v[15] = jnp.full((1, 128), -1, jnp.int32)
    ask_s[...] = fr_v[...].reshape(16, 128).astype(F32).astype(BF)
    ask_r[mine, :] = ask_s[...]
    pl.semaphore_wait(barrier, 22)
    asks = [send(ask_s, ask_r.at[mine, :], (p, line)) for p in peers]

    loads["base"].wait()
    base_b[0:112, :] = base_v[0:112, :].astype(BF)
    tail = jnp.concatenate([base_v[112:120, :], jnp.zeros((8, Q), F32)], axis=0)
    base_b[112:128, :] = tail.astype(BF)
    loads["slot"].wait()
    sl = slot_v[...]
    o = lax.shift_right_logical(sl * 4370, 16)
    lo = o & 7
    rel = (z - lax.shift_right_logical(lo, 1) + 4) & 3
    other = (lo & 1) ^ core
    place = (other * 4 + rel) * 256 + lax.shift_right_logical(o, 3) * 16 + (sl - o * 15)
    row256 = lax.broadcasted_iota(jnp.int32, (256, KD), 0)

    def heat(b, _):
        hot[pl.ds(pl.multiple_of(b * 256, 256), 256), :] = jnp.where(row256 == place - b * 256, 1.0, 0.0).astype(BF)
        return 0

    lax.fori_loop(0, 8, heat, 0)

    for a in asks:
        a.wait_recv()
    lane = lax.broadcasted_iota(jnp.int32, (256, 128), 1)
    wanted = jnp.where(lane == ctg * 8 + line, ask_r[...].astype(F32), 0.0).astype(BF)
    wanted = jnp.dot(wanted, jnp.ones((128, 128), BF), preferred_element_type=F32)
    pick = jnp.where(wanted == lane.astype(F32), 1.0, 0.0).astype(BF)
    found = jnp.dot(pick, base_b[...], preferred_element_type=F32).astype(BF)
    for i in range(NC):
        val_s[i] = found[:, i * 128 : (i + 1) * 128]
    vals = []
    for p in peers:
        theirs = pl.ds(pl.multiple_of(p * 16, 16), 16)
        vals.append(send(val_s.at[:, theirs, :], slots.at[:, 0, mine, :], (p, line)))
    for i in range(NC):
        slots[i, 0, mine, :] = val_s[i, mine, :]

    for name in ("sens0", "sens1", "sens2", "sens3"):
        loads[name].wait()
    sens_v[3, 3] = jnp.zeros((128, 128), BF)
    sens_x[0, :, :, 0:128] = sens_v[y]
    sens_x[1, :, :, 0:128] = sens_v[:, x]
    loads["lodf"].wait()
    loads["dual"].wait()

    def weigh(i, _):
        rows = pl.ds(pl.multiple_of(i * 32, 32), 32)
        w_v[rows, 0:ML] = (dual_v[rows, :].astype(F32) * lodf_v[rows, :].astype(F32)).astype(BF)
        w_v[rows, ML:MP] = jnp.zeros((32, MP - ML), BF)
        return 0

    lax.fori_loop(0, KD // 32, weigh, 0)
    loads["rating"].wait()
    rows_r = lax.broadcasted_iota(jnp.int32, (16, 128), 0)
    limit = jnp.sum(jnp.where((rows_r == ctg) & (rows_r < 15), rating_v[...], 0.0), axis=0, keepdims=True)

    for v in vals:
        v.wait_recv()

    far, near, relayed = [None] * NC, [None] * NC, [None] * NC

    def gather(i):
        far[i] = [send(slots.at[i, 0], slots.at[i, e], (ctg, mod4(z + e) * 2 + core)) for e in (2, 1, 3)]
        near[i] = send(slots.at[i, 0], slots.at[i, 4], sib)

    def relay(i):
        for c in far[i]:
            c.wait_recv()
        relayed[i] = send(slots.at[i, 1:4], slots.at[i, 5:8], sib)

    def collect(i):
        tn = (((0,), (0,)), ((), ()))
        a = lax.dot_general(slots[i, 0:4].reshape(1024, 128), hot[0:1024, :], tn, preferred_element_type=F32)
        near[i].wait_recv()
        relayed[i].wait_recv()
        b = lax.dot_general(slots[i, 4:8].reshape(1024, 128), hot[1024:2048, :], tn, preferred_element_type=F32)
        of_b[i] = (a + b).astype(BF)

    sum1, sum2 = [[[], []] for _ in range(NC)], [[[], []] for _ in range(NC)]

    def shifts(i):
        for e in (2, 1, 3, 0):
            g = mod4(y + e)
            cols = pl.ds(pl.multiple_of(g * 512, 512), 512)
            got = jnp.dot(of_b[i], w_v[:, cols], preferred_element_type=F32).astype(BF)
            for t in range(4):
                tile = got[:, t * 128 : (t + 1) * 128]
                s1[i, 0, t, g] = tile[0:HR]
                s1[i, 1, g, t] = tile[HR:128]
            if e:
                sum1[i][1].append(send(s1.at[i, 1, g], r1.at[i, 1, e - 1], along(1, e)))
        for e in (2, 1, 3):
            sum1[i][0].append(send(s1.at[i, 0, mod4(x + e)], r1.at[i, 0, e - 1], along(0, e)))

    def second(i):
        for h in (1, 0):
            for c in sum1[i][h]:
                c.wait_recv()
            total = s1[i, h, here[h]].astype(F32)
            for e in range(3):
                total = total + r1[i, h, e].astype(F32)
            t2[i, h] = total
            s2[i, h] = total.astype(BF)
            for e in (2, 1, 3):
                sum2[i][h].append(
                    send(s2.at[i, h, mod4(here[1 - h] + e)], r2.at[i, h, e - 1], along(1 - h, e)))

    gathered = [[[], []] for _ in range(NC)]

    def excess(i):
        for h in (1, 0):
            for c in sum2[i][h]:
                c.wait_recv()
            total = t2[i, h, here[1 - h]]
            for e in range(3):
                total = total + r2[i, h, e].astype(F32)
            lanes = at128(here[h])
            ex[i, h, :, lanes] = (total - jnp.clip(total, -limit, limit)).astype(BF)
            for e in (2, 1, 3):
                gathered[i][h].append(send(ex.at[i, h, :, lanes], ex.at[i, h, :, lanes], along(h, e)))

    zsum, last = [None] * NC, [[] for _ in range(NC)]

    def cut(i):
        both = []
        for h in range(2):
            for c in gathered[i][h]:
                c.wait_recv()
            both.append(jnp.dot(ex[i, h], sens_x[h].reshape(512, 512), preferred_element_type=F32))
        both = jnp.concatenate(both, axis=0)
        for e in range(4):
            flat = both[:, e * 128 : (e + 1) * 128].T.reshape(8, 16, 128)
            part[i, e] = flat
            zs[i, e] = flat.astype(BF)
        zsum[i] = []
        for e in (4, 5, 3, 2, 6, 7, 1):
            p = lax.rem(line + e, 8)
            zsum[i].append(send(zs.at[i, :, p], zr.at[i, e - 1], (ctg, p)))

    def cut_last(i):
        for c in zsum[i]:
            c.wait_recv()
        total = part[i, :, line]
        for e in range(7):
            total = total + zr[i, e].astype(F32)
        v_v[i] = total
        for h in range(2):
            for e in (2, 1, 3):
                last[i].append(send(v_v.at[i, e], rr.at[i, h, e - 1], along(1 - h, -e)))

    def finish(i):
        for c in last[i]:
            c.wait_recv()
        lane_o = lax.broadcasted_iota(jnp.int32, (16, 128), 1)
        total = v_v[i, 0]
        for e in range(3):
            total = total + jnp.where(lane_o < HR, rr[i, 0, e], rr[i, 1, e])
        out_ref[:, i * 128 : (i + 1) * 128] = total

    for i in range(NC):
        gather(i)
    swaps = []
    for e in (2, 1, 3):
        swaps.append(send(sens_v.at[mod4(y + e)], sens_x.at[0, :, :, e * 128 : (e + 1) * 128], along(1, e)))
        swaps.append(send(sens_v.at[:, mod4(x + e)], sens_x.at[1, :, :, e * 128 : (e + 1) * 128], along(0, e)))
    old = len(sent)
    relay(0)
    collect(0)
    relay(1)
    shifts(0)
    collect(1)
    relay(2)
    shifts(1)
    collect(2)
    shifts(2)
    for i in range(NC):
        second(i)
    drain(sent[:old])
    old = len(sent) - 6
    for i in range(NC):
        excess(i)
    for c in swaps:
        c.wait_recv()
    drain(sent[:old])
    for i in range(NC):
        cut(i)
    for i in range(NC):
        cut_last(i)
    for i in range(NC):
        finish(i)
    drain(sent)


def per_device(base_flow, lodf, dual, rating, sens, fetch_rows, ctg_slot):
    hbm = pl.BlockSpec(memory_space=pl.ANY)
    vm = pltpu.VMEM
    return pl.pallas_call(
        kernel,
        out_shape=jax.ShapeDtypeStruct((16, Q), F32),
        in_specs=[hbm] * 7,
        out_specs=pl.BlockSpec(memory_space=pltpu.VMEM),
        scratch_shapes=[
            vm((16, 1, 128), jnp.int32), vm((1, KD), jnp.int32), vm((120, Q), F32), vm((128, Q), BF),
            vm((KD, ML), BF), vm((KD, ML), BF), vm((16, 128), F32), vm((4, 4, 128, 128), BF), vm((2, 4, 128, 512), BF),
            vm((KD, MP), BF), vm((2048, KD), BF),
            vm((16, 128), BF), vm((256, 128), BF), vm((NC, 256, 128), BF), vm((NC, 8, 256, 128), BF), vm((NC, 128, KD), BF),
            vm((NC, 2, 4, 4, HR, 128), BF), vm((NC, 2, 3, 4, HR, 128), BF), vm((NC, 2, 4, HR, 128), F32),
            vm((NC, 2, 4, HR, 128), BF), vm((NC, 2, 3, HR, 128), BF), vm((NC, 2, HR, 512), BF),
            vm((NC, 4, 8, 16, 128), F32), vm((NC, 4, 8, 16, 128), BF), vm((NC, 7, 4, 16, 128), BF), vm((NC, 4, 16, 128), F32), vm((NC, 2, 3, 16, 128), F32),
            pltpu.SemaphoreType.DMA((10,)), pltpu.SemaphoreType.DMA((N_SEM,)), pltpu.SemaphoreType.DMA((N_SEM,)),
        ],
        compiler_params=pltpu.CompilerParams(
            collective_id=0, has_side_effects=True, vmem_limit_bytes=56 * 1024 * 1024
        ),
    )(fetch_rows.transpose(2, 0, 1), ctg_slot[None, :], base_flow.T, lodf.T, dual.T, rating.reshape(15, 128),
      sens.reshape(15, 128, 128))


def solution(mesh):
    in_specs = (
        P(None, ("ctg", "line")),
        P("line", "ctg"),
        P("line", "ctg"),
        P("line"),
        P("line", "ctg"),
        P("ctg", None, None),
        P("ctg"),
    )
    out_specs = P(("ctg", "line"), None)
    return jax.shard_map(
        per_device, mesh=mesh, in_specs=in_specs, out_specs=out_specs, check_vma=False
    )
```

```python
import jax
import jax.numpy as jnp
from jax import lax
from jax.experimental import pallas as pl
from jax.experimental.pallas import tpu as pltpu
from jax.sharding import PartitionSpec as P

MESH = pl.DeviceIdType.MESH
BF = jnp.bfloat16
F32 = jnp.float32
Q = 384
NC = 3
HR = 64
KD = 960
ML = 1920
MP = 2048
N_SEM = 176


def mod4(v):
    return lax.rem(v + 4, 4)


def at128(i):
    return pl.ds(pl.multiple_of(i * 128, 128), 128)


def kernel(
    fr_h, slot_h, base_h, lodf_h, dual_h, rating_h, sens_h, out_ref,
    fr_v, slot_v, base_v, base_b, lodf_v, dual_v, rating_v, sens_v, sens_x, w_v, hot,
    ask_s, ask_r, val_s, slots, of_b,
    s1, r1, t2, s2, r2, ex, part, zs, zr, v_v, rr,
    load_sem, send_sem, recv_sem,
):
    ctg = lax.axis_index("ctg")
    line = lax.axis_index("line")
    y, x = lax.div(ctg, 4), lax.rem(ctg, 4)
    z, core = lax.div(line, 2), lax.rem(line, 2)
    here = (x, y)
    sent, ended = [], set()

    def send(src, dst, to):
        i = len(sent)
        copy = pltpu.make_async_remote_copy(
            src_ref=src, dst_ref=dst, send_sem=send_sem.at[i], recv_sem=recv_sem.at[i],
            device_id=to, device_id_type=MESH,
        )
        sent.append(copy)
        copy.start()
        return copy

    def drain(copies):
        for c in copies:
            if id(c) not in ended:
                c.wait_send()
                ended.add(id(c))

    def along(axis, d):
        return (y * 4 + mod4(x + d), line) if axis == 0 else (mod4(y + d) * 4 + x, line)

    sib = (ctg, z * 2 + 1 - core)
    steps = sorted(((a, b) for a in range(4) for b in range(4) if a or b), key=lambda ab: -(min(ab[0], 4 - ab[0]) + min(ab[1], 4 - ab[1])))
    peers = [mod4(y + a) * 4 + mod4(x + b) for a, b in steps]

    loads = {}
    plan = [("fr", fr_h, fr_v.at[0:15]), ("base", base_h, base_v), ("slot", slot_h, slot_v),
            ("lodf", lodf_h, lodf_v), ("dual", dual_h, dual_v),
            ("sens0", sens_h.at[0:4], sens_v.at[0]), ("sens1", sens_h.at[4:8], sens_v.at[1]),
            ("sens2", sens_h.at[8:12], sens_v.at[2]), ("sens3", sens_h.at[12:15], sens_v.at[3, 0:3]),
            ("rating", rating_h, rating_v.at[0:15])]
    for i, (name, src, dst) in enumerate(plan):
        loads[name] = pltpu.make_async_copy(src, dst, load_sem.at[i])
        loads[name].start()

    barrier = pltpu.get_barrier_semaphore()
    for p in peers:
        pl.semaphore_signal(barrier, inc=1, device_id=(p, line), device_id_type=MESH)
    for e in range(1, 8):
        pl.semaphore_signal(barrier, inc=1, device_id=(ctg, lax.rem(line + e, 8)), device_id_type=MESH)

    mine = pl.ds(pl.multiple_of(ctg * 16, 16), 16)
    loads["fr"].wait()
    fr_v[15] = jnp.full((1, 128), -1, jnp.int32)
    ask_s[...] = fr_v[...].reshape(16, 128).astype(F32).astype(BF)
    ask_r[mine, :] = ask_s[...]
    pl.semaphore_wait(barrier, 22)
    asks = [send(ask_s, ask_r.at[mine, :], (p, line)) for p in peers]

    loads["base"].wait()
    base_b[0:112, :] = base_v[0:112, :].astype(BF)
    tail = jnp.concatenate([base_v[112:120, :], jnp.zeros((8, Q), F32)], axis=0)
    base_b[112:128, :] = tail.astype(BF)
    loads["slot"].wait()
    sl = slot_v[...]
    o = lax.shift_right_logical(sl * 4370, 16)
    lo = o & 7
    rel = (z - lax.shift_right_logical(lo, 1) + 4) & 3
    other = (lo & 1) ^ core
    place = (other * 4 + rel) * 256 + lax.shift_right_logical(o, 3) * 16 + (sl - o * 15)
    row256 = lax.broadcasted_iota(jnp.int32, (256, KD), 0)

    def heat(b, _):
        hot[pl.ds(pl.multiple_of(b * 256, 256), 256), :] = jnp.where(row256 == place - b * 256, 1.0, 0.0).astype(BF)
        return 0

    lax.fori_loop(0, 8, heat, 0)

    for a in asks:
        a.wait_recv()
    lane = lax.broadcasted_iota(jnp.int32, (256, 128), 1)
    wanted = jnp.where(lane == ctg * 8 + line, ask_r[...].astype(F32), 0.0).astype(BF)
    wanted = jnp.dot(wanted, jnp.ones((128, 128), BF), preferred_element_type=F32)
    pick = jnp.where(wanted == lane.astype(F32), 1.0, 0.0).astype(BF)
    found = jnp.dot(pick, base_b[...], preferred_element_type=F32).astype(BF)
    for i in range(NC):
        val_s[i] = found[:, i * 128 : (i + 1) * 128]
    vals = []
    for p in peers:
        theirs = pl.ds(pl.multiple_of(p * 16, 16), 16)
        vals.append(send(val_s.at[0, theirs, :], slots.at[0, 0, mine, :], (p, line)))
    rest = []
    for p in peers:
        theirs = pl.ds(pl.multiple_of(p * 16, 16), 16)
        rest.append(send(val_s.at[1:3, theirs, :], slots.at[1:3, 0, mine, :], (p, line)))
    for i in range(NC):
        slots[i, 0, mine, :] = val_s[i, mine, :]

    for name in ("sens0", "sens1", "sens2", "sens3"):
        loads[name].wait()
    sens_v[3, 3] = jnp.zeros((128, 128), BF)
    sens_x[0, :, :, 0:128] = sens_v[y]
    sens_x[1, :, :, 0:128] = sens_v[:, x]
    loads["lodf"].wait()
    loads["dual"].wait()

    def weigh(i, _):
        rows = pl.ds(pl.multiple_of(i * 32, 32), 32)
        w_v[rows, 0:ML] = (dual_v[rows, :].astype(F32) * lodf_v[rows, :].astype(F32)).astype(BF)
        w_v[rows, ML:MP] = jnp.zeros((32, MP - ML), BF)
        return 0

    lax.fori_loop(0, KD // 32, weigh, 0)
    loads["rating"].wait()
    rows_r = lax.broadcasted_iota(jnp.int32, (16, 128), 0)
    limit = jnp.sum(jnp.where((rows_r == ctg) & (rows_r < 15), rating_v[...], 0.0), axis=0, keepdims=True)

    for v in vals:
        v.wait_recv()

    far, near, relayed = [None] * NC, [None] * NC, [None] * NC

    def gather(i):
        far[i] = [send(slots.at[i, 0], slots.at[i, e], (ctg, mod4(z + e) * 2 + core)) for e in (2, 1, 3)]
        near[i] = send(slots.at[i, 0], slots.at[i, 4], sib)

    def relay(i):
        for c in far[i]:
            c.wait_recv()
        relayed[i] = send(slots.at[i, 1:4], slots.at[i, 5:8], sib)

    def collect(i):
        tn = (((0,), (0,)), ((), ()))
        a = lax.dot_general(slots[i, 0:4].reshape(1024, 128), hot[0:1024, :], tn, preferred_element_type=F32)
        near[i].wait_recv()
        relayed[i].wait_recv()
        b = lax.dot_general(slots[i, 4:8].reshape(1024, 128), hot[1024:2048, :], tn, preferred_element_type=F32)
        of_b[i] = (a + b).astype(BF)

    sum1, sum2 = [[[], []] for _ in range(NC)], [[[], []] for _ in range(NC)]

    def shifts(i):
        for e in (2, 1, 3, 0):
            g = mod4(y + e)
            cols = pl.ds(pl.multiple_of(g * 512, 512), 512)
            got = jnp.dot(of_b[i], w_v[:, cols], preferred_element_type=F32).astype(BF)
            for t in range(4):
                tile = got[:, t * 128 : (t + 1) * 128]
                s1[i, 0, t, g] = tile[0:HR]
                s1[i, 1, g, t] = tile[HR:128]
            if e:
                sum1[i][1].append(send(s1.at[i, 1, g], r1.at[i, 1, e - 1], along(1, e)))
        for e in (2, 1, 3):
            sum1[i][0].append(send(s1.at[i, 0, mod4(x + e)], r1.at[i, 0, e - 1], along(0, e)))

    def second(i):
        for h in (1, 0):
            for c in sum1[i][h]:
                c.wait_recv()
            total = s1[i, h, here[h]].astype(F32)
            for e in range(3):
                total = total + r1[i, h, e].astype(F32)
            t2[i, h] = total
            s2[i, h] = total.astype(BF)
            for e in (2, 1, 3):
                sum2[i][h].append(
                    send(s2.at[i, h, mod4(here[1 - h] + e)], r2.at[i, h, e - 1], along(1 - h, e)))

    gathered = [[[], []] for _ in range(NC)]

    def excess(i):
        for h in (1, 0):
            for c in sum2[i][h]:
                c.wait_recv()
            total = t2[i, h, here[1 - h]]
            for e in range(3):
                total = total + r2[i, h, e].astype(F32)
            lanes = at128(here[h])
            ex[i, h, :, lanes] = (total - jnp.clip(total, -limit, limit)).astype(BF)
            for e in (2, 1, 3):
                gathered[i][h].append(send(ex.at[i, h, :, lanes], ex.at[i, h, :, lanes], along(h, e)))

    zsum, last = [None] * NC, [[] for _ in range(NC)]

    def cut(i):
        both = []
        for h in range(2):
            for c in gathered[i][h]:
                c.wait_recv()
            both.append(jnp.dot(ex[i, h], sens_x[h].reshape(512, 512), preferred_element_type=F32))
        both = jnp.concatenate(both, axis=0)
        for e in range(4):
            flat = both[:, e * 128 : (e + 1) * 128].T.reshape(8, 16, 128)
            part[i, e] = flat
            zs[i, e] = flat.astype(BF)
        zsum[i] = []
        for e in (4, 5, 3, 2, 6, 7, 1):
            p = lax.rem(line + e, 8)
            zsum[i].append(send(zs.at[i, :, p], zr.at[i, e - 1], (ctg, p)))

    def cut_last(i):
        for c in zsum[i]:
            c.wait_recv()
        total = part[i, :, line]
        for e in range(7):
            total = total + zr[i, e].astype(F32)
        v_v[i] = total
        for h in range(2):
            for e in (2, 1, 3):
                last[i].append(send(v_v.at[i, e], rr.at[i, h, e - 1], along(1 - h, -e)))

    def finish(i):
        for c in last[i]:
            c.wait_recv()
        lane_o = lax.broadcasted_iota(jnp.int32, (16, 128), 1)
        total = v_v[i, 0]
        for e in range(3):
            total = total + jnp.where(lane_o < HR, rr[i, 0, e], rr[i, 1, e])
        out_ref[:, i * 128 : (i + 1) * 128] = total

    gather(0)
    for v in rest:
        v.wait_recv()
    gather(1)
    gather(2)
    swaps = []
    for e in (2, 1, 3):
        swaps.append(send(sens_v.at[mod4(y + e)], sens_x.at[0, :, :, e * 128 : (e + 1) * 128], along(1, e)))
        swaps.append(send(sens_v.at[:, mod4(x + e)], sens_x.at[1, :, :, e * 128 : (e + 1) * 128], along(0, e)))
    old = len(sent)
    relay(0)
    collect(0)
    relay(1)
    shifts(0)
    collect(1)
    relay(2)
    shifts(1)
    collect(2)
    shifts(2)
    for i in range(NC):
        second(i)
    drain(sent[:old])
    old = len(sent) - 6
    for i in range(NC):
        excess(i)
    for c in swaps:
        c.wait_recv()
    drain(sent[:old])
    for i in range(NC):
        cut(i)
    for i in range(NC):
        cut_last(i)
    for i in range(NC):
        finish(i)
    drain(sent)


def per_device(base_flow, lodf, dual, rating, sens, fetch_rows, ctg_slot):
    hbm = pl.BlockSpec(memory_space=pl.ANY)
    vm = pltpu.VMEM
    return pl.pallas_call(
        kernel,
        out_shape=jax.ShapeDtypeStruct((16, Q), F32),
        in_specs=[hbm] * 7,
        out_specs=pl.BlockSpec(memory_space=pltpu.VMEM),
        scratch_shapes=[
            vm((16, 1, 128), jnp.int32), vm((1, KD), jnp.int32), vm((120, Q), F32), vm((128, Q), BF),
            vm((KD, ML), BF), vm((KD, ML), BF), vm((16, 128), F32), vm((4, 4, 128, 128), BF), vm((2, 4, 128, 512), BF),
            vm((KD, MP), BF), vm((2048, KD), BF),
            vm((16, 128), BF), vm((256, 128), BF), vm((NC, 256, 128), BF), vm((NC, 8, 256, 128), BF), vm((NC, 128, KD), BF),
            vm((NC, 2, 4, 4, HR, 128), BF), vm((NC, 2, 3, 4, HR, 128), BF), vm((NC, 2, 4, HR, 128), F32),
            vm((NC, 2, 4, HR, 128), BF), vm((NC, 2, 3, HR, 128), BF), vm((NC, 2, HR, 512), BF),
            vm((NC, 4, 8, 16, 128), F32), vm((NC, 4, 8, 16, 128), BF), vm((NC, 7, 4, 16, 128), BF), vm((NC, 4, 16, 128), F32), vm((NC, 2, 3, 16, 128), F32),
            pltpu.SemaphoreType.DMA((10,)), pltpu.SemaphoreType.DMA((N_SEM,)), pltpu.SemaphoreType.DMA((N_SEM,)),
        ],
        compiler_params=pltpu.CompilerParams(
            collective_id=0, has_side_effects=True, vmem_limit_bytes=56 * 1024 * 1024
        ),
    )(fetch_rows.transpose(2, 0, 1), ctg_slot[None, :], base_flow.T, lodf.T, dual.T, rating.reshape(15, 128),
      sens.reshape(15, 128, 128))


def solution(mesh):
    in_specs = (
        P(None, ("ctg", "line")),
        P("line", "ctg"),
        P("line", "ctg"),
        P("line"),
        P("line", "ctg"),
        P("ctg", None, None),
        P("ctg"),
    )
    out_specs = P(("ctg", "line"), None)
    return jax.shard_map(
        per_device, mesh=mesh, in_specs=in_specs, out_specs=out_specs, check_vma=False
    )
```
